32 devices in a mesh: groups: 2 (over y), tensor: 4 (over z), dp: 4 (over x, core).
Axes of the slice: x: 2, y: 2, z: 4, core: 2. Of those that a mesh axis runs over, the one named last changes fastest.
Arguments:
- tokens: bfloat16 [1024, 16384], P(('groups', 'dp'), 'tensor'), parts along dimension 0, may hold values from -6 to 6
- out_grad: bfloat16 [1024, 16384], P(('groups', 'dp'), 'tensor'), parts along dimension 0, may hold values from -6 to 6
- gate_weight: bfloat16 [16384, 8192], P('dp', 'tensor'), may hold values from -0.046875 to 0.046875
- up_weight: bfloat16 [16384, 8192], P('dp', 'tensor'), may hold values from -0.046875 to 0.046875
- down_weight: bfloat16 [8192, 16384], P('dp', 'tensor'), may hold values from -0.0625 to 0.0625
- in_up: bfloat16 [16384, 64], P('tensor'), may hold values from -0.046875 to 0.046875
- out_up: bfloat16 [8192, 64], P('tensor'), may hold values from -0.0625 to 0.0625
- in_down: bfloat16 [8192, 64], P('tensor'), may hold values from -0.0625 to 0.0625
- out_down: bfloat16 [16384, 64], P('tensor'), may hold values from -0.046875 to 0.046875
- doc_ids: int32 [1024], P(('groups', 'dp')), parts along dimension 0, may hold values from 0 to 7, as said below
Outputs:
- log_up: float32 [16, 64, 64], P(('groups', 'dp')), parts along dimension 0
- log_down: float32 [16, 64, 64], P(('groups', 'dp')), parts along dimension 0
The draws below stay inside these ranges and needn't reach their ends.
There are 2 independent parts, one for each index of `groups`. The reference program is written for one: setup_inputs(seed, part) draws one part's arguments, and reference() takes and returns one part's arrays. A program takes and returns all parts, laid end to end along the dimension named above; an argument that names none is the same for every part. Nothing has to cross between parts.
Inputs may be any that keep to these rules, and one draw needn't show every extreme that they name: `doc_ids`: the tokens of dp index b form the aligned block b of 128 tokens; its ids never fall and take every value from b * 2 to b * 2 + 1.
All inputs are finite; a program needn't handle non-finite values.
Results may differ from the reference program's by a relative error of at most 0.003.
Values may be sent and summed in bfloat16 or wider, within the bound.
A program may use at most 512 MiB of HBM per device.

```python
import jax
import jax.numpy as jnp
from jax import lax

D = 16384
FF = 8192
RANK = 64
TOK_DP = 128
DOCS_DP = 2
TOKENS = 512
NDOCS = 8


def draw_doc_ids(key, part):
    key = jax.random.fold_in(key, 7)
    blocks = TOKENS // TOK_DP
    block_keys = jax.random.split(key, blocks)
    positions = jnp.arange(TOK_DP, dtype=jnp.int32)

    def one_block(block_key, block):
        shuffled = jax.random.permutation(block_key, TOK_DP - 1)
        boundaries = jnp.sort(shuffled[:DOCS_DP - 1]) + 1
        local_ids = jnp.sum((positions[:, None] >= boundaries[None, :]).astype(jnp.int32), axis=1)
        return local_ids + block * DOCS_DP
    doc_values = jax.vmap(one_block)(block_keys, jnp.arange(blocks, dtype=jnp.int32))
    return doc_values.reshape(-1).astype(jnp.int32)


def shard_levels(key, dims, cuts, least, high):
    factor_of = 1.0
    for dim, parts in cuts:
        heights = jax.random.uniform(jax.random.fold_in(jax.random.fold_in(key, 6), dim), (parts,), jnp.float32, least / len(cuts), high / len(cuts))
        factor_of = factor_of * jnp.repeat(jnp.exp(heights), dims[dim] // parts).reshape((-1,) + (1,) * (len(dims) - 1 - dim))
    return factor_of


def gaussian(key, shape, spread, reach, pieces=(), kind=jnp.bfloat16):
    drawn = jax.random.normal(key, shape, jnp.float32) * spread
    if len(pieces) > 0:
        drawn = shard_levels(key, shape, pieces, -0.22, 0.18) * drawn
    return jnp.clip(drawn, min=-reach, max=reach).astype(kind)


def setup_inputs(seed: int = 0, part: int = 0) -> dict:
    key_list = jax.random.split(jax.random.key(seed), 11)
    own_keys = jax.random.split(jax.random.fold_in(key_list[10], part), 11)
    return {
        "tokens": gaussian(own_keys[0], (TOKENS, D), 1.0, 6.0, ((0, 4), (1, 4))),
        "out_grad": gaussian(own_keys[1], (TOKENS, D), 1.0, 6.0, ((0, 4), (1, 4))),
        "gate_weight": gaussian(key_list[2], (D, FF), D ** -0.5, 0.046875, ((0, 4), (1, 4))),
        "up_weight": gaussian(key_list[3], (D, FF), D ** -0.5, 0.046875, ((0, 4), (1, 4))),
        "down_weight": gaussian(key_list[4], (FF, D), FF ** -0.5, 0.0625, ((0, 4), (1, 4))),
        "in_up": gaussian(key_list[5], (D, RANK), D ** -0.5, 0.046875, ((0, 4),)),
        "out_up": gaussian(key_list[6], (FF, RANK), FF ** -0.5, 0.0625, ((0, 4),)),
        "in_down": gaussian(key_list[7], (FF, RANK), FF ** -0.5, 0.0625, ((0, 4),)),
        "out_down": gaussian(key_list[8], (D, RANK), D ** -0.5, 0.046875, ((0, 4),)),
        "doc_ids": draw_doc_ids(jax.random.fold_in(jax.random.fold_in(key_list[10], part), 71), part),
    }


def document_gram(onehot, left, right):
    return jnp.einsum("td,tr,ts->drs", onehot, left, right, precision=lax.Precision.HIGHEST)


def reference(tokens, out_grad, gate_weight, up_weight, down_weight, in_up, out_up, in_down, out_down, doc_ids):
    gate = jnp.dot(tokens, gate_weight, preferred_element_type=jnp.float32)
    up = jnp.dot(tokens, up_weight, preferred_element_type=jnp.float32)
    hidden = (jax.nn.silu(gate) * up).astype(jnp.bfloat16)
    hidden_grad = lax.dot_general(out_grad, down_weight, (((1,), (1,)), ((), ())), preferred_element_type=jnp.float32)
    up_grad = (hidden_grad * jax.nn.silu(gate)).astype(jnp.bfloat16)
    a_up = jnp.dot(tokens, in_up, preferred_element_type=jnp.float32)
    b_up = jnp.dot(up_grad, out_up, preferred_element_type=jnp.float32)
    a_down = jnp.dot(hidden, in_down, preferred_element_type=jnp.float32)
    b_down = jnp.dot(out_grad, out_down, preferred_element_type=jnp.float32)
    onehot = (doc_ids[:, None] == jnp.arange(NDOCS, dtype=jnp.int32)[None, :]).astype(jnp.float32)
    return document_gram(onehot, a_up, b_up), document_gram(onehot, a_down, b_down)
```

```python
import jax
import jax.numpy as jnp
from jax import lax
from jax.sharding import PartitionSpec as P

DOCS_DP = 2


def document_gram(onehot, left, right):
    return jnp.einsum("td,tr,ts->drs", onehot, left, right, precision=lax.Precision.HIGHEST)


def make_shards(n_tensor, n_dp):
    per = n_tensor // n_dp

    def shards(
        tokens, out_grad, gate_weight, up_weight, down_weight, in_up, out_up, in_down, out_down, doc_ids
    ):
        rows = tokens.shape[0]
        a_up_part = jnp.dot(tokens, in_up, preferred_element_type=jnp.float32)
        b_down_part = jnp.dot(out_grad, out_down, preferred_element_type=jnp.float32)
        grads = lax.all_gather(out_grad, "dp", axis=0, tiled=True)
        hg_part = lax.dot_general(
            grads, down_weight, (((1,), (1,)), ((), ())), preferred_element_type=jnp.float32
        )
        units = hg_part.shape[1] // per
        hg_part = hg_part.reshape(n_dp, rows, per, units).transpose(2, 0, 1, 3)
        hg_part = hg_part.reshape(per * n_dp * rows, units)
        hg = lax.psum_scatter(hg_part, "tensor", scatter_dimension=0, tiled=True)
        hidden_grad = lax.ppermute(
            hg,
            ("tensor", "dp"),
            [
                (t * n_dp + d, (d * per + t // n_dp) * n_dp + t % n_dp)
                for t in range(n_tensor)
                for d in range(n_dp)
            ],
        )
        whole = lax.all_gather(tokens, "tensor", axis=1, tiled=True)
        mine = lax.all_to_all(whole, "dp", split_axis=1, concat_axis=0, tiled=True)
        gate_part = jnp.dot(mine, gate_weight, preferred_element_type=jnp.float32)
        gate = lax.psum_scatter(gate_part, "dp", scatter_dimension=0, tiled=True)
        up_part = jnp.dot(mine, up_weight, preferred_element_type=jnp.float32)
        up = lax.psum_scatter(up_part, "dp", scatter_dimension=0, tiled=True)
        activated = jax.nn.silu(gate)
        hidden = (activated * up).astype(jnp.bfloat16)
        up_grad = (hidden_grad * activated).astype(jnp.bfloat16)
        b_up_part = jnp.dot(up_grad, out_up, preferred_element_type=jnp.float32)
        a_down_part = jnp.dot(hidden, in_down, preferred_element_type=jnp.float32)
        first_doc = lax.axis_index("dp") * DOCS_DP
        local_docs = doc_ids - first_doc
        onehot = (local_docs[:, None] == jnp.arange(DOCS_DP, dtype=jnp.int32)[None, :]).astype(
            jnp.float32
        )
        a_up, b_up, a_down, b_down = lax.psum(
            (a_up_part, b_up_part, a_down_part, b_down_part), "tensor"
        )
        log_up = document_gram(onehot, a_up, b_up)
        log_down = document_gram(onehot, a_down, b_down)
        return (log_up, log_down)

    return shards


def solution(mesh):
    placed = (
        P(("groups", "dp"), "tensor"),
        P(("groups", "dp"), "tensor"),
        P("dp", "tensor"),
        P("dp", "tensor"),
        P("dp", "tensor"),
        P("tensor", None),
        P("tensor", None),
        P("tensor", None),
        P("tensor", None),
        P(("groups", "dp")),
    )
    return jax.shard_map(
        make_shards(mesh.shape["tensor"], mesh.shape["dp"]),
        mesh=mesh,
        in_specs=placed,
        out_specs=(P(("groups", "dp"), None, None), P(("groups", "dp"), None, None)),
        check_vma=False,
    )
```

```python
import functools

import jax
import jax.numpy as jnp
from jax import lax
from jax.experimental import pallas as pl
from jax.experimental.pallas import tpu as pltpu
from jax.sharding import PartitionSpec as P

DOCS_DP = 2
CHUNKS = 2
SLOTS = 4
PAIR_TYPE = jnp.float32
DOWN_SLOTS = 2
MESH = pl.DeviceIdType.MESH


def document_gram(onehot, left, right):
    return jnp.einsum("td,tr,ts->drs", onehot, left, right, precision=lax.Precision.HIGHEST)


def kernel(
    n_t, n_d,
    tok, og, gate_w, up_w, down_w, in_up, out_up, in_down, out_down,
    fac,
    ring, mine, grads, hg_send, hg_recv, part, sib_recv, pair_send, pair_recv, wbuf, dbuf, fbuf,
    w_sem, d_sem, up_s, dn_s, ring_r, feat_s, feat_r, og_s, og_f, og_r, og_l,
    hg_s, hg_r, sib_s, sib_r, pair_s, pair_r, f_s, f_r,
):
    per = n_t // n_d
    rows, feats = tok.shape
    crow = rows // CHUNKS
    units = out_up.shape[0]
    n_j, _, tile = part.shape[1:]
    half = n_d // 2
    n_h, tile_h = down_w.shape[0] // dbuf.shape[1], dbuf.shape[1]
    g, t, d = lax.axis_index("groups"), lax.axis_index("tensor"), lax.axis_index("dp")

    def remote(src, dst, ss, rs, tt, dd):
        return pltpu.make_async_remote_copy(
            src_ref=src, dst_ref=dst, send_sem=ss, recv_sem=rs,
            device_id=(g, tt, dd), device_id_type=MESH,
        )

    def w_copy(which, j, slot):
        ref = gate_w if which == 0 else up_w
        cols = pl.ds(pl.multiple_of(j * tile, tile), tile)
        return pltpu.make_async_copy(ref.at[:, cols], wbuf.at[slot], w_sem.at[slot])

    def d_copy(h, slot):
        r = pl.ds(pl.multiple_of(h * tile_h, tile_h), tile_h)
        return pltpu.make_async_copy(down_w.at[r, :], dbuf.at[slot], d_sem.at[slot])

    for h in range(min(DOWN_SLOTS, n_h)):
        d_copy(h, h).start()
    for i in range(min(SLOTS, 2 * n_j)):
        w_copy(i % 2, i // 2, i).start()
    own_og = pl.ds(pl.multiple_of(d * rows, rows), rows)
    og_local = pltpu.make_async_copy(og, grads.at[own_og, :], og_l.at[0])
    og_local.start()

    barrier = pltpu.get_barrier_semaphore()

    def greet(i, carry):
        @pl.when(i != t * n_d + d)
        def _():
            pl.semaphore_signal(
                barrier, inc=1, device_id=(g, i // n_d, i % n_d), device_id_type=MESH
            )
        return carry

    lax.fori_loop(0, n_t * n_d, greet, 0)
    pl.semaphore_wait(barrier, n_t * n_d - 1)

    def block(s, c):
        return ring.at[s, pl.ds(c * crow, crow), :]

    def own(c):
        return tok.at[pl.ds(c * crow, crow), :]

    def ring_up(src, s, c):
        return remote(src, block(s, c), up_s.at[s, c], ring_r.at[s, c], t + 1, d)

    def ring_dn(src, s, c):
        return remote(src, block(s, c), dn_s.at[s, c], ring_r.at[s, c], t - 1, d)

    def landing(dd, s, c):
        r = pl.ds(pl.multiple_of(dd * rows + c * crow, crow), crow)
        return mine.at[r, pl.ds(pl.multiple_of((s % per) * feats, 128), feats)]

    def feat_remote(src, s, c):
        return remote(
            src, landing(d, s, c), feat_s.at[s, c], feat_r.at[d, s % per, c], t, s // per
        )

    def feat_local(src, s, c):
        return pltpu.make_async_copy(src, landing(d, s, c), feat_r.at[d, s % per, c])

    def hand_over(src, s, c):
        @pl.when(s // per != d)
        def _():
            feat_remote(src, s, c).start()

        @pl.when(s // per == d)
        def _():
            feat_local(src, s, c).start()

    for c in range(CHUNKS):
        @pl.when(t < n_t - 1)
        def _():
            ring_up(own(c), t, c).start()

        @pl.when(t > 0)
        def _():
            ring_dn(own(c), t, c).start()

        hand_over(own(c), t, c)

    sib = d + 1 - 2 * (d % 2)

    def og_rows(dd):
        return grads.at[pl.ds(pl.multiple_of(dd * rows, rows), rows), :]

    og_first = [remote(og, og_rows(d), og_s.at[0], og_r.at[d], t, sib)]
    for m in range(1, n_d // 2):
        peer = (d + 2 * m) % n_d
        og_first.append(remote(og, og_rows(d), og_s.at[m], og_r.at[d], t, peer))
    for copy in og_first:
        copy.start()

    fbuf[t, 0] = jnp.dot(tok[...], in_up[...], preferred_element_type=jnp.float32)
    fbuf[t, 1] = jnp.dot(og[...], out_down[...], preferred_element_type=jnp.float32)

    def fac_copy(late, m):
        to = (t + m) % n_t
        return remote(
            fbuf.at[t, pl.ds(2 * late, 2)], fbuf.at[t, pl.ds(2 * late, 2)],
            f_s.at[late, m], f_r.at[late, t], to, d,
        )

    def fac_wait(late, m):
        s = (t + m) % n_t
        remote(
            fbuf.at[s, pl.ds(2 * late, 2)], fbuf.at[s, pl.ds(2 * late, 2)],
            f_s.at[late, m], f_r.at[late, s], t, d,
        ).wait_recv()

    def step(k):
        for c in range(CHUNKS):
            s = t - k

            @pl.when(s >= 0)
            def _():
                ring_up(block(s, c), s, c).wait_recv()

                @pl.when(t < n_t - 1)
                def _():
                    ring_up(block(s, c), s, c).start()

                hand_over(block(s, c), s, c)

            r = t + k

            @pl.when(r < n_t)
            def _():
                ring_dn(block(r, c), r, c).wait_recv()

                @pl.when(t > 0)
                def _():
                    ring_dn(block(r, c), r, c).start()

                hand_over(block(r, c), r, c)

    def hidden_tile(h, carry):
        slot = h % DOWN_SLOTS
        d_copy(h, slot).wait()
        out = lax.dot_general(
            grads[...], dbuf[slot], (((1,), (1,)), ((), ())), preferred_element_type=jnp.float32
        )
        hg_send[:, pl.ds(pl.multiple_of(h * tile_h, tile_h), tile_h)] = out.astype(jnp.bfloat16)

        @pl.when(h + DOWN_SLOTS < n_h)
        def _():
            d_copy(h + DOWN_SLOTS, slot).start()
        return carry

    def og_arrive():
        forwards = []
        for m in range(1, n_d // 2):
            src = (d + n_d - 2 * m) % n_d
            remote(og, og_rows(src), og_s.at[m], og_r.at[src], t, sib).wait_recv()
            f = remote(og_rows(src), og_rows(src), og_f.at[m], og_r.at[src], t, sib)
            f.start()
            forwards.append(f)
        og_local.wait()
        remote(og, og_rows(sib), og_s.at[0], og_r.at[sib], t, sib).wait_recv()
        for m in range(1, n_d // 2):
            src = (sib + n_d - 2 * m) % n_d
            remote(og, og_rows(src), og_s.at[m], og_r.at[src], t, sib).wait_recv()
        return forwards

    if n_t <= 8:
        forwards = None
        for k in range(1, n_t):
            step(k)
            if k == 1:
                forwards = og_arrive()
            lo, hi = (k - 1) * n_h // (n_t - 1), k * n_h // (n_t - 1)
            lax.fori_loop(lo, hi, hidden_tile, 0)
    else:
        lax.fori_loop(1, n_t, lambda k, carry: (step(k), carry)[1], 0)
        forwards = og_arrive()
        lax.fori_loop(0, n_h, hidden_tile, 0)

    def hg_src(i, b):
        return hg_send.at[pl.ds(b * rows, rows), pl.ds(i * units, units)]

    def hg_remote(i, b):
        return remote(
            hg_src(i, b), hg_recv.at[t], hg_s.at[i, b], hg_r.at[t], d * per + i, b
        )

    def hg_self(i, b):
        return (d * per + i == t) & (d == b)

    for i in range(per):
        for b in range(n_d):
            @pl.when(jnp.logical_not(hg_self(i, b)))
            def _():
                hg_remote(i, b).start()

            @pl.when(hg_self(i, b))
            def _():
                pltpu.make_async_copy(hg_src(i, b), hg_recv.at[t], hg_r.at[t]).start()

    for m in range(1, n_t):
        fac_copy(0, m).start()

    for dd in range(n_d):
        for p in range(per):
            for c in range(CHUNKS):
                s = p
                remote(
                    landing(dd, s, c), landing(dd, s, c), feat_s.at[0, c], feat_r.at[dd, p, c],
                    t, d,
                ).wait_recv()

    def block_rows(dd):
        return pl.ds(pl.multiple_of(dd * rows, rows), rows)

    def sib_copy(which, j, m):
        to = (sib + 2 * m) % n_d
        return remote(
            part.at[which, j, block_rows(to), :], sib_recv.at[which, j, m],
            sib_s.at[which, j, m], sib_r.at[which, j, m], t, sib,
        )

    def pair_copy(which, j, m):
        return remote(
            pair_send.at[which, j, m - 1], pair_recv.at[which, j, m - 1],
            pair_s.at[which, j, m - 1], pair_r.at[which, j, m - 1], t, (d + 2 * m) % n_d,
        )

    def pair_up(which, j):
        for m in range(half):
            sib_copy(which, j, m).wait_recv()
            dd = block_rows((d + 2 * m) % n_d)
            total = part[which, j, dd, :] + sib_recv[which, j, m]
            if m == 0:
                part[which, j, dd, :] = total
            else:
                pair_send[which, j, m - 1] = total.astype(pair_send.dtype)
                pair_copy(which, j, m).start()

    def project(j, carry):
        for which in range(2):
            item = 2 * j + which
            slot = item % SLOTS
            w_copy(which, j, slot).wait()
            part[which, j] = jnp.dot(
                mine[...], wbuf[slot], preferred_element_type=jnp.float32
            )
            for m in range(half):
                sib_copy(which, j, m).start()

            @pl.when(item + SLOTS < 2 * n_j)
            def _():
                w_copy(which, j + SLOTS // 2, slot).start()

        @pl.when(j > 0)
        def _():
            for which in range(2):
                pair_up(which, j - 1)
        return carry

    lax.fori_loop(0, n_j, project, 0)
    for which in range(2):
        pair_up(which, n_j - 1)

    for s in range(n_t):
        remote(hg_src(0, 0), hg_recv.at[s], hg_s.at[0, 0], hg_r.at[s], t, d).wait_recv()
    fbuf[t, 2] = jnp.zeros_like(fbuf[t, 2])
    fbuf[t, 3] = jnp.zeros_like(fbuf[t, 3])

    def finish(j, carry):
        sums = []
        for which in range(2):
            total = part[which, j, block_rows(d), :]
            for m in range(1, half):
                pair_copy(which, j, m).wait_recv()
                total = total + pair_recv[which, j, m - 1].astype(jnp.float32)
            sums.append(total)
        gate, up = sums
        cols = pl.ds(pl.multiple_of(j * tile, tile), tile)
        activated = gate / (1.0 + jnp.exp(-gate))
        hidden = (activated * up).astype(jnp.bfloat16)
        hidden_grad = hg_recv[0, :, cols].astype(jnp.float32)
        for s in range(1, n_t):
            hidden_grad = hidden_grad + hg_recv[s, :, cols].astype(jnp.float32)
        up_grad = hidden_grad * activated
        high = up_grad.astype(jnp.bfloat16)
        low = (up_grad - high.astype(jnp.float32)).astype(jnp.bfloat16)
        weight = out_up[cols, :]
        fbuf[t, 2] += jnp.dot(high, weight, preferred_element_type=jnp.float32) + jnp.dot(
            low, weight, preferred_element_type=jnp.float32
        )
        fbuf[t, 3] += jnp.dot(hidden, in_down[cols, :], preferred_element_type=jnp.float32)
        return carry

    lax.fori_loop(0, n_j, finish, 0)
    for m in range(1, n_t):
        fac_copy(1, m).start()
    for late in range(2):
        for m in range(1, n_t):
            fac_wait(late, m)
    fac[...] = jnp.sum(fbuf[...], axis=0)

    for late in range(2):
        for m in range(1, n_t):
            fac_copy(late, m).wait_send()

    def part_done(j, carry):
        for which in range(2):
            for m in range(half):
                sib_copy(which, j, m).wait_send()
            for m in range(1, half):
                pair_copy(which, j, m).wait_send()
        return carry

    lax.fori_loop(0, n_j, part_done, 0)
    for i in range(per):
        for b in range(n_d):
            @pl.when(jnp.logical_not(hg_self(i, b)))
            def _():
                hg_remote(i, b).wait_send()
    for copy in og_first:
        copy.wait_send()
    for copy in forwards:
        copy.wait_send()

    def ring_done(s, carry):
        for c in range(CHUNKS):
            @pl.when((s <= t) & (t < n_t - 1))
            def _():
                ring_up(block(s, c), s, c).wait_send()

            @pl.when((s >= t) & (t > 0))
            def _():
                ring_dn(block(s, c), s, c).wait_send()

            @pl.when(s // per != d)
            def _():
                feat_remote(block(s, c), s, c).wait_send()
        return carry

    lax.fori_loop(0, n_t, ring_done, 0)


def make_shards(n_t, n_d):
    def shards(
        tokens, out_grad, gate_weight, up_weight, down_weight, in_up, out_up, in_down, out_down, doc_ids
    ):
        rows, feats = tokens.shape
        deep, units = gate_weight.shape
        block_units = down_weight.shape[0]
        rank = in_up.shape[1]
        tile = min(256, units)
        tile_h = min(256, block_units)
        n_j = units // tile
        per, half = n_t // n_d, n_d // 2
        bf16, f32 = jnp.bfloat16, jnp.float32
        vmem = pl.BlockSpec(memory_space=pltpu.VMEM)
        hbm = pl.BlockSpec(memory_space=pl.ANY)
        dma = pltpu.SemaphoreType.DMA
        fac = pl.pallas_call(
            functools.partial(kernel, n_t, n_d),
            out_shape=jax.ShapeDtypeStruct((4, rows, rank), f32),
            in_specs=[vmem, vmem, hbm, hbm, hbm, vmem, vmem, vmem, vmem],
            out_specs=vmem,
            scratch_shapes=[
                pltpu.VMEM((n_t, rows, feats), bf16),
                pltpu.VMEM((n_d * rows, deep), bf16),
                pltpu.VMEM((n_d * rows, feats), bf16),
                pltpu.VMEM((n_d * rows, block_units), bf16),
                pltpu.VMEM((n_t, rows, units), bf16),
                pltpu.VMEM((2, n_j, n_d * rows, tile), f32),
                pltpu.VMEM((2, n_j, half, rows, tile), f32),
                pltpu.VMEM((2, n_j, half - 1, rows, tile), PAIR_TYPE),
                pltpu.VMEM((2, n_j, half - 1, rows, tile), PAIR_TYPE),
                pltpu.VMEM((SLOTS, deep, tile), bf16),
                pltpu.VMEM((DOWN_SLOTS, tile_h, feats), bf16),
                pltpu.VMEM((n_t, 4, rows, rank), f32),
                dma((SLOTS,)), dma((DOWN_SLOTS,)),
                dma((n_t, CHUNKS)), dma((n_t, CHUNKS)), dma((n_t, CHUNKS)),
                dma((n_t, CHUNKS)), dma((n_d, per, CHUNKS)),
                dma((n_d,)), dma((n_d,)), dma((n_d,)), dma((1,)),
                dma((per, n_d)), dma((n_t,)),
                dma((2, n_j, half)), dma((2, n_j, half)),
                dma((2, n_j, half - 1)), dma((2, n_j, half - 1)),
                dma((2, n_t)), dma((2, n_t)),
            ],
            compiler_params=pltpu.CompilerParams(
                collective_id=0, has_side_effects=True, vmem_limit_bytes=58 * 2**20
            ),
        )(tokens, out_grad, gate_weight, up_weight, down_weight, in_up, out_up, in_down, out_down)
        a_up, b_down, b_up, a_down = fac[0], fac[1], fac[2], fac[3]
        local_docs = doc_ids - lax.axis_index("dp") * DOCS_DP
        onehot = (local_docs[:, None] == jnp.arange(DOCS_DP, dtype=jnp.int32)[None, :]).astype(
            jnp.float32
        )
        return document_gram(onehot, a_up, b_up), document_gram(onehot, a_down, b_down)

    return shards


def solution(mesh):
    placed = (
        P(("groups", "dp"), "tensor"),
        P(("groups", "dp"), "tensor"),
        P("dp", "tensor"),
        P("dp", "tensor"),
        P("dp", "tensor"),
        P("tensor", None),
        P("tensor", None),
        P("tensor", None),
        P("tensor", None),
        P(("groups", "dp")),
    )
    return jax.shard_map(
        make_shards(mesh.shape["tensor"], mesh.shape["dp"]),
        mesh=mesh,
        in_specs=placed,
        out_specs=(P(("groups", "dp"), None, None), P(("groups", "dp"), None, None)),
        check_vma=False,
    )
```

```python
import functools

import jax
import jax.numpy as jnp
from jax import lax
from jax.experimental import pallas as pl
from jax.experimental.pallas import tpu as pltpu
from jax.sharding import PartitionSpec as P

DOCS_DP = 2
CHUNKS = 4
SLOTS = 4
PAIR_TYPE = jnp.float32
DOWN_SLOTS = 2
MESH = pl.DeviceIdType.MESH
ROWS_BY_ROWS = (((1,), (1,)), ((), ()))


def document_gram(onehot, left, right):
    return jnp.einsum("td,tr,ts->drs", onehot, left, right, precision=lax.Precision.HIGHEST)


def kernel(
    n_t, n_d,
    tok, og, gate_w, up_w, down_w, in_up, out_up, in_down, out_down,
    fac,
    ring, mine, grads, hg_send, hg_recv, part, sib_recv, pair_send, pair_recv, wbuf, dbuf, fbuf,
    w_sem, d_sem, up_s, dn_s, ring_r, feat_s, feat_r, og_s, og_f, og_r, og_l,
    hg_s, hg_r, sib_s, sib_r, pair_s, pair_r, f_s, f_r,
):
    per = n_t // n_d
    rows, feats = tok.shape
    crow = rows // CHUNKS
    units = out_up.shape[1]
    n_j, _, tile = part.shape[1:]
    half = n_d // 2
    n_h, tile_h = down_w.shape[0] // dbuf.shape[1], dbuf.shape[1]
    g, t, d = lax.axis_index("groups"), lax.axis_index("tensor"), lax.axis_index("dp")

    def remote(src, dst, ss, rs, tt, dd):
        return pltpu.make_async_remote_copy(
            src_ref=src, dst_ref=dst, send_sem=ss, recv_sem=rs,
            device_id=(g, tt, dd), device_id_type=MESH,
        )

    def w_copy(which, j, slot):
        ref = gate_w if which == 0 else up_w
        cols = pl.ds(pl.multiple_of(j * tile, tile), tile)
        return pltpu.make_async_copy(ref.at[:, cols], wbuf.at[slot], w_sem.at[slot])

    def d_copy(h, slot):
        r = pl.ds(pl.multiple_of(h * tile_h, tile_h), tile_h)
        return pltpu.make_async_copy(down_w.at[r, :], dbuf.at[slot], d_sem.at[slot])

    for h in range(min(DOWN_SLOTS, n_h)):
        d_copy(h, h).start()
    for i in range(min(SLOTS, 2 * n_j)):
        w_copy(i % 2, i // 2, i).start()
    own_og = pl.ds(pl.multiple_of(d * rows, rows), rows)
    og_local = pltpu.make_async_copy(og, grads.at[own_og, :], og_l.at[0])
    og_local.start()

    barrier = pltpu.get_barrier_semaphore()

    def greet(i, carry):
        @pl.when(i != t * n_d + d)
        def _():
            pl.semaphore_signal(
                barrier, inc=1, device_id=(g, i // n_d, i % n_d), device_id_type=MESH
            )
        return carry

    lax.fori_loop(0, n_t * n_d, greet, 0)
    pl.semaphore_wait(barrier, n_t * n_d - 1)

    def block(s, c):
        return ring.at[s, pl.ds(c * crow, crow), :]

    def own(c):
        return tok.at[pl.ds(c * crow, crow), :]

    def ring_up(src, s, c):
        return remote(src, block(s, c), up_s.at[s, c], ring_r.at[s, c], t + 1, d)

    def ring_dn(src, s, c):
        return remote(src, block(s, c), dn_s.at[s, c], ring_r.at[s, c], t - 1, d)

    def landing(dd, s, c):
        r = pl.ds(pl.multiple_of(dd * rows + c * crow, crow), crow)
        return mine.at[r, pl.ds(pl.multiple_of((s % per) * feats, 128), feats)]

    def feat_remote(src, s, c):
        return remote(
            src, landing(d, s, c), feat_s.at[s, c], feat_r.at[d, s % per, c], t, s // per
        )

    def feat_local(src, s, c):
        return pltpu.make_async_copy(src, landing(d, s, c), feat_r.at[d, s % per, c])

    def hand_over(src, s, c):
        @pl.when(s // per != d)
        def _():
            feat_remote(src, s, c).start()

        @pl.when(s // per == d)
        def _():
            feat_local(src, s, c).start()

    for c in range(CHUNKS):
        @pl.when(t < n_t - 1)
        def _():
            ring_up(own(c), t, c).start()

        @pl.when(t > 0)
        def _():
            ring_dn(own(c), t, c).start()

        hand_over(own(c), t, c)

    sib = d + 1 - 2 * (d % 2)

    def og_rows(dd):
        return grads.at[pl.ds(pl.multiple_of(dd * rows, rows), rows), :]

    og_first = [remote(og, og_rows(d), og_s.at[0], og_r.at[d], t, sib)]
    for m in range(1, n_d // 2):
        peer = (d + 2 * m) % n_d
        og_first.append(remote(og, og_rows(d), og_s.at[m], og_r.at[d], t, peer))
    for copy in og_first:
        copy.start()

    fbuf[t, 0] = lax.dot_general(
        tok[...], in_up[...], ROWS_BY_ROWS, preferred_element_type=jnp.float32
    )
    fbuf[t, 1] = lax.dot_general(
        og[...], out_down[...], ROWS_BY_ROWS, preferred_element_type=jnp.float32
    )

    def fac_copy(late, m):
        to = (t + m) % n_t
        return remote(
            fbuf.at[t, pl.ds(2 * late, 2)], fbuf.at[t, pl.ds(2 * late, 2)],
            f_s.at[late, m], f_r.at[late, t], to, d,
        )

    def fac_wait(late, m):
        s = (t + m) % n_t
        remote(
            fbuf.at[s, pl.ds(2 * late, 2)], fbuf.at[s, pl.ds(2 * late, 2)],
            f_s.at[late, m], f_r.at[late, s], t, d,
        ).wait_recv()

    def step(k):
        for c in range(CHUNKS):
            s = t - k

            @pl.when(s >= 0)
            def _():
                ring_up(block(s, c), s, c).wait_recv()

                @pl.when(t < n_t - 1)
                def _():
                    ring_up(block(s, c), s, c).start()

                hand_over(block(s, c), s, c)

            r = t + k

            @pl.when(r < n_t)
            def _():
                ring_dn(block(r, c), r, c).wait_recv()

                @pl.when(t > 0)
                def _():
                    ring_dn(block(r, c), r, c).start()

                hand_over(block(r, c), r, c)

    def hidden_tile(h, carry):
        slot = h % DOWN_SLOTS
        d_copy(h, slot).wait()
        out = lax.dot_general(
            grads[...], dbuf[slot], (((1,), (1,)), ((), ())), preferred_element_type=jnp.float32
        )
        hg_send[:, pl.ds(pl.multiple_of(h * tile_h, tile_h), tile_h)] = out.astype(jnp.bfloat16)

        @pl.when(h + DOWN_SLOTS < n_h)
        def _():
            d_copy(h + DOWN_SLOTS, slot).start()
        return carry

    def og_arrive():
        forwards = []
        for m in range(1, n_d // 2):
            src = (d + n_d - 2 * m) % n_d
            remote(og, og_rows(src), og_s.at[m], og_r.at[src], t, sib).wait_recv()
            f = remote(og_rows(src), og_rows(src), og_f.at[m], og_r.at[src], t, sib)
            f.start()
            forwards.append(f)
        og_local.wait()
        remote(og, og_rows(sib), og_s.at[0], og_r.at[sib], t, sib).wait_recv()
        for m in range(1, n_d // 2):
            src = (sib + n_d - 2 * m) % n_d
            remote(og, og_rows(src), og_s.at[m], og_r.at[src], t, sib).wait_recv()
        return forwards

    if n_t <= 8:
        forwards = None
        for k in range(1, n_t):
            step(k)
            if k == 1:
                forwards = og_arrive()
            lo, hi = (k - 1) * n_h // (n_t - 1), k * n_h // (n_t - 1)
            lax.fori_loop(lo, hi, hidden_tile, 0)
    else:
        lax.fori_loop(1, n_t, lambda k, carry: (step(k), carry)[1], 0)
        forwards = og_arrive()
        lax.fori_loop(0, n_h, hidden_tile, 0)

    def hg_src(i, b):
        return hg_send.at[pl.ds(b * rows, rows), pl.ds(i * units, units)]

    def hg_remote(i, b):
        return remote(
            hg_src(i, b), hg_recv.at[t], hg_s.at[i, b], hg_r.at[t], d * per + i, b
        )

    def hg_self(i, b):
        return (d * per + i == t) & (d == b)

    for i in range(per):
        for b in range(n_d):
            @pl.when(jnp.logical_not(hg_self(i, b)))
            def _():
                hg_remote(i, b).start()

            @pl.when(hg_self(i, b))
            def _():
                pltpu.make_async_copy(hg_src(i, b), hg_recv.at[t], hg_r.at[t]).start()

    for m in range(1, n_t):
        fac_copy(0, m).start()

    for dd in range(n_d):
        for p in range(per):
            for c in range(CHUNKS):
                s = p
                remote(
                    landing(dd, s, c), landing(dd, s, c), feat_s.at[0, c], feat_r.at[dd, p, c],
                    t, d,
                ).wait_recv()

    def block_rows(dd):
        return pl.ds(pl.multiple_of(dd * rows, rows), rows)

    def sib_copy(which, j, m):
        to = (sib + 2 * m) % n_d
        return remote(
            part.at[which, j, block_rows(to), :], sib_recv.at[which, j, m],
            sib_s.at[which, j, m], sib_r.at[which, j, m], t, sib,
        )

    def pair_copy(which, j, m):
        return remote(
            pair_send.at[which, j, m - 1], pair_recv.at[which, j, m - 1],
            pair_s.at[which, j, m - 1], pair_r.at[which, j, m - 1], t, (d + 2 * m) % n_d,
        )

    def pair_up(which, j):
        for m in range(half):
            sib_copy(which, j, m).wait_recv()
            dd = block_rows((d + 2 * m) % n_d)
            total = part[which, j, dd, :] + sib_recv[which, j, m]
            if m == 0:
                part[which, j, dd, :] = total
            else:
                pair_send[which, j, m - 1] = total.astype(pair_send.dtype)
                pair_copy(which, j, m).start()

    def project(j, carry):
        for which in range(2):
            item = 2 * j + which
            slot = item % SLOTS
            w_copy(which, j, slot).wait()
            part[which, j] = jnp.dot(
                mine[...], wbuf[slot], preferred_element_type=jnp.float32
            )
            for m in range(half):
                sib_copy(which, j, m).start()

            @pl.when(item + SLOTS < 2 * n_j)
            def _():
                w_copy(which, j + SLOTS // 2, slot).start()

        @pl.when(j > 0)
        def _():
            for which in range(2):
                pair_up(which, j - 1)
        return carry

    lax.fori_loop(0, n_j, project, 0)
    for which in range(2):
        pair_up(which, n_j - 1)

    for s in range(n_t):
        remote(hg_src(0, 0), hg_recv.at[s], hg_s.at[0, 0], hg_r.at[s], t, d).wait_recv()
    fbuf[t, 2] = jnp.zeros_like(fbuf[t, 2])
    fbuf[t, 3] = jnp.zeros_like(fbuf[t, 3])

    def finish(j, carry):
        sums = []
        for which in range(2):
            total = part[which, j, block_rows(d), :]
            for m in range(1, half):
                pair_copy(which, j, m).wait_recv()
                total = total + pair_recv[which, j, m - 1].astype(jnp.float32)
            sums.append(total)
        gate, up = sums
        cols = pl.ds(pl.multiple_of(j * tile, tile), tile)
        activated = gate / (1.0 + jnp.exp(-gate))
        hidden = (activated * up).astype(jnp.bfloat16)
        hidden_grad = hg_recv[0, :, cols].astype(jnp.float32)
        for s in range(1, n_t):
            hidden_grad = hidden_grad + hg_recv[s, :, cols].astype(jnp.float32)
        up_grad = hidden_grad * activated
        high = up_grad.astype(jnp.bfloat16)
        low = (up_grad - high.astype(jnp.float32)).astype(jnp.bfloat16)
        weight = out_up[:, cols]
        fbuf[t, 2] += lax.dot_general(
            high, weight, ROWS_BY_ROWS, preferred_element_type=jnp.float32
        ) + lax.dot_general(low, weight, ROWS_BY_ROWS, preferred_element_type=jnp.float32)
        fbuf[t, 3] += lax.dot_general(
            hidden, in_down[:, cols], ROWS_BY_ROWS, preferred_element_type=jnp.float32
        )
        return carry

    lax.fori_loop(0, n_j, finish, 0)
    for m in range(1, n_t):
        fac_copy(1, m).start()
    for late in range(2):
        for m in range(1, n_t):
            fac_wait(late, m)
    fac[...] = jnp.sum(fbuf[...], axis=0)

    for late in range(2):
        for m in range(1, n_t):
            fac_copy(late, m).wait_send()

    def part_done(j, carry):
        for which in range(2):
            for m in range(half):
                sib_copy(which, j, m).wait_send()
            for m in range(1, half):
                pair_copy(which, j, m).wait_send()
        return carry

    lax.fori_loop(0, n_j, part_done, 0)
    for i in range(per):
        for b in range(n_d):
            @pl.when(jnp.logical_not(hg_self(i, b)))
            def _():
                hg_remote(i, b).wait_send()
    for copy in og_first:
        copy.wait_send()
    for copy in forwards:
        copy.wait_send()

    def ring_done(s, carry):
        for c in range(CHUNKS):
            @pl.when((s <= t) & (t < n_t - 1))
            def _():
                ring_up(block(s, c), s, c).wait_send()

            @pl.when((s >= t) & (t > 0))
            def _():
                ring_dn(block(s, c), s, c).wait_send()

            @pl.when(s // per != d)
            def _():
                feat_remote(block(s, c), s, c).wait_send()
        return carry

    lax.fori_loop(0, n_t, ring_done, 0)


def make_shards(n_t, n_d):
    def shards(
        tokens, out_grad, gate_weight, up_weight, down_weight, in_up, out_up, in_down, out_down, doc_ids
    ):
        rows, feats = tokens.shape
        deep, units = gate_weight.shape
        block_units = down_weight.shape[0]
        rank = in_up.shape[1]
        tile = min(256, units)
        tile_h = min(256, block_units)
        n_j = units // tile
        per, half = n_t // n_d, n_d // 2
        bf16, f32 = jnp.bfloat16, jnp.float32
        vmem = pl.BlockSpec(memory_space=pltpu.VMEM)
        hbm = pl.BlockSpec(memory_space=pl.ANY)
        dma = pltpu.SemaphoreType.DMA
        fac = pl.pallas_call(
            functools.partial(kernel, n_t, n_d),
            out_shape=jax.ShapeDtypeStruct((4, rows, rank), f32),
            in_specs=[vmem, vmem, hbm, hbm, hbm, vmem, vmem, vmem, vmem],
            out_specs=vmem,
            scratch_shapes=[
                pltpu.VMEM((n_t, rows, feats), bf16),
                pltpu.VMEM((n_d * rows, deep), bf16),
                pltpu.VMEM((n_d * rows, feats), bf16),
                pltpu.VMEM((n_d * rows, block_units), bf16),
                pltpu.VMEM((n_t, rows, units), bf16),
                pltpu.VMEM((2, n_j, n_d * rows, tile), f32),
                pltpu.VMEM((2, n_j, half, rows, tile), f32),
                pltpu.VMEM((2, n_j, half - 1, rows, tile), PAIR_TYPE),
                pltpu.VMEM((2, n_j, half - 1, rows, tile), PAIR_TYPE),
                pltpu.VMEM((SLOTS, deep, tile), bf16),
                pltpu.VMEM((DOWN_SLOTS, tile_h, feats), bf16),
                pltpu.VMEM((n_t, 4, rows, rank), f32),
                dma((SLOTS,)), dma((DOWN_SLOTS,)),
                dma((n_t, CHUNKS)), dma((n_t, CHUNKS)), dma((n_t, CHUNKS)),
                dma((n_t, CHUNKS)), dma((n_d, per, CHUNKS)),
                dma((n_d,)), dma((n_d,)), dma((n_d,)), dma((1,)),
                dma((per, n_d)), dma((n_t,)),
                dma((2, n_j, half)), dma((2, n_j, half)),
                dma((2, n_j, half - 1)), dma((2, n_j, half - 1)),
                dma((2, n_t)), dma((2, n_t)),
            ],
            compiler_params=pltpu.CompilerParams(
                collective_id=0, has_side_effects=True, vmem_limit_bytes=58 * 2**20
            ),
        )(
            tokens, out_grad, gate_weight, up_weight, down_weight,
            in_up.T, out_up.T, in_down.T, out_down.T,
        )
        a_up, b_down, b_up, a_down = fac[0], fac[1], fac[2], fac[3]
        local_docs = doc_ids - lax.axis_index("dp") * DOCS_DP
        onehot = (local_docs[:, None] == jnp.arange(DOCS_DP, dtype=jnp.int32)[None, :]).astype(
            jnp.float32
        )
        return document_gram(onehot, a_up, b_up), document_gram(onehot, a_down, b_down)

    return shards


def solution(mesh):
    placed = (
        P(("groups", "dp"), "tensor"),
        P(("groups", "dp"), "tensor"),
        P("dp", "tensor"),
        P("dp", "tensor"),
        P("dp", "tensor"),
        P("tensor", None),
        P("tensor", None),
        P("tensor", None),
        P("tensor", None),
        P(("groups", "dp")),
    )
    return jax.shard_map(
        make_shards(mesh.shape["tensor"], mesh.shape["dp"]),
        mesh=mesh,
        in_specs=placed,
        out_specs=(P(("groups", "dp"), None, None), P(("groups", "dp"), None, None)),
        check_vma=False,
    )
```
